512 devices in a mesh: owner: 64 (over x, z, core), kv: 8 (over y).
Axes of the slice: x: 4, y: 8, z: 8, core: 2. Of those that a mesh axis runs over, the one named last changes fastest.
Arguments:
- queries: bfloat16 [2048, 8192], P(('owner', 'kv')), may hold values from -30 to 30
- paths: int32 [2048, 3], P('owner'), may hold values from 0 to 63, all different within a row; in each aligned block of 32 rows (0 to 31, 32 to 63, ...) at most 8 rows name the same one
- node_owner: int32 [64], replicated, may hold values from 0 to 63, each once
- node_len: int32 [64], replicated, may hold values from 1 to 512, 8192 in all
- suf_len: int32 [2048], P('owner'), may hold values from 1 to 64, 65536 in all
- prefix_kv: bfloat16 [64, 2, 512, 1024], P('owner', None, None, 'kv'), may hold values from -30 to 30
- suffix_key_value: bfloat16 [2048, 2, 64, 1024], P('owner', None, None, 'kv'), may hold values from -30 to 30
- fresh_key_value: bfloat16 [2048, 2, 1024], P('owner', None, 'kv'), may hold values from -30 to 30
Outputs:
- attended: bfloat16 [2048, 8192], P(('owner', 'kv'))
The draws below stay inside these ranges and needn't reach their ends.
Inputs may be any that keep to these rules, and one draw needn't show every extreme that they name: `paths`: the 3 nodes of a request are distinct. Among the 32 requests of one owner index (aligned blocks of rows), no node is named by more than 8 of them, a bound that some block reaches.
All inputs are finite; a program needn't handle non-finite values. No bound on the sum of `suf_len` on one device may be relied on, other than what follows from the above.
Results may differ from the reference program's by a relative error of at most 0.0022.
Values may be sent and summed in bfloat16 or wider, within the bound.
No kernel may reach another device: no remote copies, remote signals or barrier semaphores. Data moves between devices by JAX's collectives and lax.ppermute only.
A program may use at most 64 MiB of HBM per device.

```python
import math
import jax
import jax.numpy as jnp
import numpy as np
from jax import lax

QUERY_HEADS = 64
KEY_VALUE_HEADS = 8
HEAD_SIZE = 128
REQ_DEV = 32
NODE_LENGTH = 512
SUFFIX_LENGTH = 64
PATH = 3
REQUEST_TOTAL = 2048
PREFIX_NODES = 64
CAP = 8


def draw_queries(key, part):
    key = jax.random.fold_in(key, 11)
    base_offset = jnp.clip(jax.random.normal(key, (REQUEST_TOTAL, QUERY_HEADS * HEAD_SIZE), jnp.float32), -6.0, 6.0)
    return base_offset.astype(jnp.bfloat16)


def draw_prefix_kv(key, part):
    key = jax.random.fold_in(key, 23)
    base_offset = jnp.clip(jax.random.normal(key, (PREFIX_NODES, 2, NODE_LENGTH, KEY_VALUE_HEADS * HEAD_SIZE), jnp.float32), -6.0, 6.0)
    return base_offset.astype(jnp.bfloat16)


def draw_suffix_key_value(key, part):
    key = jax.random.fold_in(key, 37)
    base_offset = jnp.clip(jax.random.normal(key, (REQUEST_TOTAL, 2, SUFFIX_LENGTH, KEY_VALUE_HEADS * HEAD_SIZE), jnp.float32), -6.0, 6.0)
    return base_offset.astype(jnp.bfloat16)


def draw_fresh_key_value(key, part):
    key = jax.random.fold_in(key, 41)
    base_offset = jnp.clip(2.5 * jax.random.normal(key, (REQUEST_TOTAL, 2, KEY_VALUE_HEADS * HEAD_SIZE), jnp.float32), -15.0, 15.0)
    return base_offset.astype(jnp.bfloat16)


def length_profile(amount, total, bound, skew):
    loads = [(1 << 20) // math.isqrt(standing ** skew) + 1 for standing in range(2, amount + 1)]
    rest, given = total - bound - (amount - 1), [1] * (amount - 1)
    while rest > 0:
        candidates = [i for i in range(amount - 1) if given[i] < bound]
        whole, budget = sum([loads[i] for i in candidates]), rest
        for i in candidates:
            addition = min(bound - given[i], max(1, budget * loads[i] // whole), rest)
            given[i] = given[i] + addition
            rest = rest - addition
    return np.array([bound] + given)


def ragged_sizes(key, amount, total, limit, slope):
    if amount == 2:
        one = jax.random.randint(key, (), max(1, total - limit), min(limit, total - 1) + 1)
        return jnp.stack([one, total - one])
    tallies = jnp.asarray(length_profile(amount, total, limit, slope), jnp.int32)
    couples = (amount - 1) // 2
    donor, receiver = tallies[1:1 + 2 * couples:2], tallies[2:2 + 2 * couples:2]
    room = jnp.minimum(donor - 1, limit - receiver)
    moved = jax.random.randint(jax.random.fold_in(key, 1), (couples,), 0, 1 << 20) % (room + 1)
    tallies = tallies.at[1:1 + 2 * couples:2].set(donor - moved).at[2:2 + 2 * couples:2].set(receiver + moved)
    return tallies[jax.random.permutation(jax.random.fold_in(key, 2), amount)]


def assign_block(rng, own, number, rows, number_of, top, most, lean):
    ranking = jax.random.permutation(rng, number_of)
    crowded, usual = portions_of(number_of, rows * top, most, lean, True), portions_of(number_of, rows * top, most, lean, False)
    places = jnp.arange(number_of)

    def named(lengths, offset_by):
        used = int((lengths > 0).sum())
        fixed = max(1, used // 4)
        shifted = fixed + (places - fixed + offset_by * (used - fixed)) % max(1, number_of - fixed)
        return jnp.zeros((number_of,), jnp.int32).at[ranking[jnp.where(places < fixed, places, shifted)]].set(jnp.asarray(lengths, jnp.int32))

    lengths = jnp.where(number % 4 == 0, named(crowded, number // 4), named(usual, number - number // 4 - 1))
    mixed = jax.random.permutation(jax.random.fold_in(own, 3), number_of)
    giver, sink = mixed[0:number_of // 2 * 2:2], mixed[1:number_of // 2 * 2:2]
    room = jnp.minimum(lengths[giver] - 1, most - lengths[sink]) // 2
    room = jnp.where((giver == ranking[0]) | (sink == ranking[0]) | (lengths[sink] == 0), 0, jnp.maximum(room, 0))
    shifted = jax.random.randint(jax.random.fold_in(own, 4), (number_of // 2,), 0, 1 << 20) % (room + 1)
    lengths = lengths.at[giver].add(-shifted).at[sink].add(shifted)
    items = jnp.searchsorted(jnp.cumsum(lengths), jnp.arange(rows * top), side="right").astype(jnp.int32)
    listing = items.reshape(top, rows).T
    listing = listing[jax.random.permutation(jax.random.fold_in(own, 1), rows)]
    offset_by = jax.random.randint(jax.random.fold_in(own, 2), (rows, 1), 0, top)
    return jnp.take_along_axis(listing, (jnp.arange(top)[None, :] + offset_by) % top, axis=1)


def portions_of(number_of, total, reach, slope, full):
    loads = [(1 << 20) // math.isqrt(standing ** slope) + 1 for standing in range(1, number_of + 1)]
    largest = reach if full else min(reach, max(-(-total // number_of), total * loads[0] // sum(loads)))
    least = 1 if total - largest >= number_of - 1 else 0
    counts, rest = [largest] + [least] * (number_of - 1), total - largest - least * (number_of - 1)
    while rest > 0:
        candidates = [i for i in range(1, number_of) if counts[i] < largest] or [i for i in range(1, number_of) if counts[i] < reach]
        whole, left = sum([loads[i] for i in candidates]), rest
        for i in candidates:
            addition = min(reach - counts[i], max(1, left * loads[i] // whole), rest)
            counts[i] = counts[i] + addition
            rest = rest - addition
    return np.array(counts)


def setup_inputs(seed: int = 0) -> dict:
    keys = jax.random.split(jax.random.key(seed), 9)
    queries = draw_queries(jax.random.fold_in(keys[8], 71), 0)
    paths_keys = jax.random.split(jax.random.fold_in(keys[1], 1), REQUEST_TOTAL // REQ_DEV)
    paths_turns = jax.random.permutation(jax.random.fold_in(keys[1], 3), REQUEST_TOTAL // REQ_DEV)
    paths = jax.vmap(lambda own, number: assign_block(jax.random.fold_in(keys[1], 2), own, number, REQ_DEV, PREFIX_NODES, PATH, CAP, 2))(paths_keys, paths_turns).reshape((REQUEST_TOTAL, PATH))
    node_owner = jax.random.permutation(keys[2], PREFIX_NODES).astype(jnp.int32)
    node_len = ragged_sizes(keys[3], PREFIX_NODES, PREFIX_NODES * NODE_LENGTH // 4, NODE_LENGTH, 2).astype(jnp.int32)
    suf_len = ragged_sizes(keys[4], REQUEST_TOTAL, REQUEST_TOTAL * SUFFIX_LENGTH // 2, SUFFIX_LENGTH, 1).astype(jnp.int32)
    prefix_kv = draw_prefix_kv(jax.random.fold_in(keys[8], 71), 0)
    suffix_key_value = draw_suffix_key_value(jax.random.fold_in(keys[8], 71), 0)
    fresh_key_value = draw_fresh_key_value(jax.random.fold_in(keys[8], 71), 0)
    return {"queries": queries, "paths": paths, "node_owner": node_owner, "node_len": node_len, "suf_len": suf_len, "prefix_kv": prefix_kv, "suffix_key_value": suffix_key_value, "fresh_key_value": fresh_key_value}


def partial_summary(query_head_rows, key_matrix, value_matrix, validity_mask):
    scores = jnp.einsum("kgd,tkd->kgt", query_head_rows, key_matrix.astype(jnp.float32)) * (HEAD_SIZE ** -0.5)
    highest = jnp.max(jnp.where(validity_mask[None, None, :], scores, -jnp.inf), axis=-1)
    weights = jnp.where(validity_mask[None, None, :], jnp.exp(scores - highest[..., None]), 0.0)
    weight_sum = jnp.sum(weights, axis=-1)
    rounded = lax.optimization_barrier(weights.astype(jnp.bfloat16)).astype(jnp.float32)
    summed = jnp.einsum("kgt,tkd->kgd", rounded, value_matrix.astype(jnp.float32))
    return highest, weight_sum, summed


def request_output(single_query, holder_row, private_suffix_cache, latest_token, suffix_count, prefix_kv, node_len):
    query_head_group = QUERY_HEADS // KEY_VALUE_HEADS
    query_head_rows = single_query.astype(jnp.float32).reshape(KEY_VALUE_HEADS, query_head_group, HEAD_SIZE)
    highs = []
    sums = []
    outputs = []
    positions = jnp.arange(NODE_LENGTH, dtype=jnp.int32)
    for level in range(PATH):
        cache_tile_block = prefix_kv[holder_row[level]]
        validity_mask = positions < node_len[holder_row[level]]
        final_output = partial_summary(query_head_rows, cache_tile_block[0].reshape(NODE_LENGTH, KEY_VALUE_HEADS, HEAD_SIZE),
                              cache_tile_block[1].reshape(NODE_LENGTH, KEY_VALUE_HEADS, HEAD_SIZE), validity_mask)
        highs.append(final_output[0])
        sums.append(final_output[1])
        outputs.append(final_output[2])
    key_matrix = jnp.concatenate([private_suffix_cache[0], latest_token[0][None, :]], axis=0).reshape(SUFFIX_LENGTH + 1, KEY_VALUE_HEADS, HEAD_SIZE)
    value_matrix = jnp.concatenate([private_suffix_cache[1], latest_token[1][None, :]], axis=0).reshape(SUFFIX_LENGTH + 1, KEY_VALUE_HEADS, HEAD_SIZE)
    validity_mask = jnp.concatenate([jnp.arange(SUFFIX_LENGTH, dtype=jnp.int32) < suffix_count, jnp.ones((1,), dtype=bool)])
    final_output = partial_summary(query_head_rows, key_matrix, value_matrix, validity_mask)
    highs.append(final_output[0])
    sums.append(final_output[1])
    outputs.append(final_output[2])
    stacked_high = jnp.stack(highs)
    stacked_sum = jnp.stack(sums)
    stacked_out = jnp.stack(outputs)
    best = jnp.max(stacked_high, axis=0)
    factors = jnp.exp(stacked_high - best[None])
    numer = jnp.sum(factors[..., None] * stacked_out, axis=0)
    denom = jnp.sum(factors * stacked_sum, axis=0)
    return (numer / denom[..., None]).reshape(QUERY_HEADS * HEAD_SIZE).astype(jnp.bfloat16)


def reference(queries, paths, node_owner, node_len, suf_len, prefix_kv, suffix_key_value, fresh_key_value):
    holders = node_owner[paths]
    batch_list = REQUEST_TOTAL // 8

    def one_batch(batch):
        query_rows, holder_rows, suffix_rows, newest_rows, count_rows = batch
        return jax.vmap(lambda a, b, c, d, e: request_output(a, b, c, d, e, prefix_kv, node_len))(
            query_rows, holder_rows, suffix_rows, newest_rows, count_rows)

    grouped = (queries.reshape(batch_list, 8, QUERY_HEADS * HEAD_SIZE), holders.reshape(batch_list, 8, PATH),
               suffix_key_value.reshape(batch_list, 8, 2, SUFFIX_LENGTH, KEY_VALUE_HEADS * HEAD_SIZE), fresh_key_value.reshape(batch_list, 8, 2, KEY_VALUE_HEADS * HEAD_SIZE),
               suf_len.reshape(batch_list, 8))
    final_output = lax.map(one_batch, grouped)
    return final_output.reshape(REQUEST_TOTAL, QUERY_HEADS * HEAD_SIZE)
```

```python
import jax
import jax.numpy as jnp
from jax import lax
from jax.experimental import pallas as pl
from jax.experimental.pallas import tpu as pltpu
from jax.sharding import Mesh
from jax.sharding import PartitionSpec as P

QUERY_HEADS = 64
KEY_VALUE_HEADS = 8
HEAD_SIZE = 128
PATH = 3
GROUP = QUERY_HEADS // KEY_VALUE_HEADS
WIDTH = GROUP * HEAD_SIZE
PAD_WIDTH = WIDTH + 128
SCALE = HEAD_SIZE ** (-0.5)
LOW = -1e30
SLOTS = 32
TILE = 8
AXES = ("x", "zh", "zl", "core", "kv")
OWNER = ("x", "zh", "zl", "core")


def nt(a, b):
    return lax.dot_general(a, b, (((1,), (1,)), ((), ())), preferred_element_type=jnp.float32)


def spread_heads(rows_ref, heads_ref):
    count = rows_ref.shape[0]
    for head in range(GROUP):
        part = rows_ref[:, head * HEAD_SIZE : (head + 1) * HEAD_SIZE].astype(jnp.float32)
        heads_ref[pl.ds(head, count, stride=GROUP), :] = part


def suffix_kernel(query_ref, cache_ref, fresh_ref, valid_ref, out_ref, high_ref, sum_ref, heads_ref):
    spread_heads(query_ref, heads_ref)
    requests, _, length, _ = cache_ref.shape
    block = 8
    rows = block * GROUP
    row_request = lax.broadcasted_iota(jnp.int32, (rows, 1), 0) // GROUP
    key_request = lax.broadcasted_iota(jnp.int32, (1, block * length), 1) // length
    fresh_request = lax.broadcasted_iota(jnp.int32, (1, requests), 1)
    own_key = row_request == key_request
    for group in range(requests // block):
        here = pl.ds(group * rows, rows)
        query = heads_ref[here, :].astype(jnp.bfloat16)
        keys = cache_ref[group * block : (group + 1) * block, 0].reshape(block * length, HEAD_SIZE)
        values = cache_ref[group * block : (group + 1) * block, 1].reshape(block * length, HEAD_SIZE)
        usable = own_key & (valid_ref[group : group + 1, :] > 0)
        scores = jnp.where(usable, nt(query, keys) * SCALE, LOW)
        newest = jnp.where(
            fresh_request == row_request + group * block, nt(query, fresh_ref[0]) * SCALE, LOW
        )
        high = jnp.maximum(
            jnp.max(scores, axis=1, keepdims=True), jnp.max(newest, axis=1, keepdims=True)
        )
        weights = jnp.exp(scores - high)
        newest_weights = jnp.exp(newest - high)
        total = jnp.sum(weights, axis=1, keepdims=True) + jnp.sum(
            newest_weights, axis=1, keepdims=True
        )
        out_ref[here, :] = jnp.dot(
            weights.astype(jnp.bfloat16), values, preferred_element_type=jnp.float32
        ) + jnp.dot(
            newest_weights.astype(jnp.bfloat16), fresh_ref[1], preferred_element_type=jnp.float32
        )
        high_ref[here, :] = jnp.broadcast_to(high, (rows, HEAD_SIZE))
        sum_ref[here, :] = jnp.broadcast_to(total, (rows, HEAD_SIZE))


def prefix_nodes(first, index_ref, count_ref, length_ref, cache_ref, heads_ref, acc, high, total):
    nodes, _, length, _ = cache_ref.shape
    columns = lax.broadcasted_iota(jnp.int32, (1, length), 1)

    def one_node(node, carry):
        place = first + node
        valid = columns < length_ref[place]

        def one_tile(tile, inner):
            where = [
                pl.multiple_of(index_ref[place, tile * TILE + slot] * GROUP, GROUP)
                for slot in range(TILE)
            ]
            query = jnp.concatenate(
                [heads_ref[pl.ds(at, GROUP), :] for at in where], axis=0
            ).astype(jnp.bfloat16)
            scores = jnp.where(valid, nt(query, cache_ref[node, 0]) * SCALE, LOW)
            part_high = jnp.max(scores, axis=1, keepdims=True)
            weights = jnp.exp(scores - part_high)
            part_sum = jnp.sum(weights, axis=1, keepdims=True)
            part_out = jnp.dot(
                weights.astype(jnp.bfloat16), cache_ref[node, 1], preferred_element_type=jnp.float32
            )
            old_high = jnp.concatenate([high[pl.ds(at, GROUP), :] for at in where], axis=0)
            old_sum = jnp.concatenate([total[pl.ds(at, GROUP), :] for at in where], axis=0)
            old_out = jnp.concatenate([acc[pl.ds(at, GROUP), :] for at in where], axis=0)
            new_high = jnp.maximum(old_high, part_high)
            old_factor = jnp.exp(old_high - new_high)
            part_factor = jnp.exp(part_high - new_high)
            new_sum = old_sum * old_factor + part_sum * part_factor
            new_out = old_out * old_factor + part_out * part_factor
            for slot, at in enumerate(where):
                rows = slice(slot * GROUP, (slot + 1) * GROUP)
                high[pl.ds(at, GROUP), :] = new_high[rows]
                total[pl.ds(at, GROUP), :] = new_sum[rows]
                acc[pl.ds(at, GROUP), :] = new_out[rows]
            return inner

        lax.fori_loop(0, (count_ref[place] + TILE - 1) // TILE, one_tile, 0)
        return carry

    lax.fori_loop(0, nodes, one_node, 0)


def prefix_kernel(
    index_ref, count_ref, length_ref, group_ref,
    query_ref, cache_a, cache_b, cache_c, cache_d, own_out, own_high, own_sum,
    sent_ref, heads_ref, acc, high, total,
):
    requests = query_ref.shape[0]
    spread_heads(query_ref, heads_ref)
    heads_ref[requests * GROUP :, :] = jnp.zeros((GROUP, HEAD_SIZE), jnp.float32)
    acc[...] = jnp.zeros(acc.shape, jnp.float32)
    total[...] = jnp.zeros(total.shape, jnp.float32)
    high[...] = jnp.full(high.shape, LOW, jnp.float32)
    own_rows = own_out.shape[0]
    own = pl.ds(pl.multiple_of(group_ref[0] * own_rows, own_rows), own_rows)
    acc[own, :] = own_out[...]
    high[own, :] = own_high[...]
    total[own, :] = own_sum[...]
    first = 0
    for cache_ref in (cache_a, cache_b, cache_c, cache_d):
        prefix_nodes(first, index_ref, count_ref, length_ref, cache_ref, heads_ref, acc, high, total)
        first += cache_ref.shape[0]
    lanes = lax.broadcasted_iota(jnp.int32, (1, 128), 1)
    stats = jnp.zeros((requests, 128), jnp.float32)
    for head in range(GROUP):
        rows = pl.ds(head, requests, stride=GROUP)
        sent_ref[:, head * HEAD_SIZE : (head + 1) * HEAD_SIZE] = acc[rows, :]
        stats = jnp.where(lanes == head, high[rows, :], stats)
        stats = jnp.where(lanes == GROUP + head, total[rows, :], stats)
    sent_ref[:, WIDTH:] = stats


def final_kernel(parts_ref, out_ref):
    sources, heads_kv = parts_ref.shape[:2]
    for group in range(heads_kv):
        stats = [parts_ref[source, group, :, WIDTH:] for source in range(sources)]
        best = stats[0]
        for stat in stats[1:]:
            best = jnp.maximum(best, stat)
        factors = [jnp.exp(jnp.minimum(stat - best, 0.0)) for stat in stats]
        for head in range(GROUP):
            columns = slice(head * HEAD_SIZE, (head + 1) * HEAD_SIZE)
            numer = 0.0
            denom = 0.0
            for source in range(sources):
                factor = factors[source][:, head : head + 1]
                numer = numer + factor * parts_ref[source, group, :, columns]
                denom = denom + factor * stats[source][:, GROUP + head : GROUP + head + 1]
            start = group * WIDTH + head * HEAD_SIZE
            out_ref[:, start : start + HEAD_SIZE] = (numer / denom).astype(jnp.bfloat16)


def shards(
    queries, paths, node_owner, node_len, suf_len, prefix_kv, suffix_key_value, fresh_key_value
):
    x, zh, zl, core, kv = [lax.axis_index(name) for name in AXES]
    xs, zhs, zls, cores, kvs = [lax.axis_size(name) for name in AXES]
    rows_each = queries.shape[0]
    request_count = paths.shape[0]
    node_ids = lax.iota(jnp.int32, node_owner.shape[0])
    with jax.named_scope("send_queries"):
        my_paths = lax.dynamic_slice_in_dim(paths, kv * rows_each, rows_each, 0)
        my_holders = jnp.sum(
            jnp.where(my_paths[:, :, None] == node_ids, node_owner, 0), axis=-1
        )
        tail = jnp.pad(my_holders, ((0, 0), (0, 128 - PATH))).astype(jnp.bfloat16)
        by_head = queries.reshape(rows_each, kvs, WIDTH).transpose(1, 0, 2)
        outgoing = jnp.concatenate(
            [by_head, jnp.broadcast_to(tail[None], (kvs, rows_each, 128))], axis=-1
        )
        outgoing = jnp.broadcast_to(outgoing[None], (zhs,) + outgoing.shape)
        received = lax.all_to_all(
            outgoing.reshape(zhs * kvs, rows_each, PAD_WIDTH),
            ("zh", "kv"), split_axis=0, concat_axis=0, tiled=True,
        ).reshape(zhs * request_count, PAD_WIDTH)
    with jax.named_scope("send_prefix"):
        own_cache = prefix_kv[0]
        swap = [(0, 1), (1, 0)]

        def over_x(block):
            return lax.all_to_all(
                jnp.broadcast_to(block[None], (xs,) + block.shape), "x",
                split_axis=0, concat_axis=0, tiled=True,
            )

        cache_a = over_x(own_cache)
        other_cache = lax.ppermute(own_cache, "zl", swap)
        cache_c = over_x(other_cache)
        cache_b = lax.ppermute(cache_a, "core", swap)
        cache_d = lax.ppermute(cache_c, "core", swap)
    with jax.named_scope("suffix"):
        own_queries = lax.dynamic_slice_in_dim(received, zh * request_count, request_count, 0)
        length = suffix_key_value.shape[2]
        valid = (lax.iota(jnp.int32, length)[None, :] < suf_len[:, None]).astype(jnp.int32)
        local = jax.ShapeDtypeStruct((request_count * GROUP, HEAD_SIZE), jnp.float32)
        own_out, own_high, own_sum = pl.pallas_call(
            suffix_kernel,
            out_shape=(local, local, local),
            scratch_shapes=[pltpu.VMEM((request_count * GROUP, HEAD_SIZE), jnp.float32)],
            compiler_params=pltpu.CompilerParams(vmem_limit_bytes=32 * 1024 * 1024),
            name="suffix_attention",
        )(
            own_queries,
            suffix_key_value,
            fresh_key_value.transpose(1, 0, 2),
            valid.reshape(-1, 8 * length),
        )
    with jax.named_scope("prefix"):
        requests = zhs * request_count
        named = received[:, WIDTH : WIDTH + PATH].astype(jnp.int32)
        base = lax.iota(jnp.int32, xs) * (zhs * zls * cores) + zh * (zls * cores)
        held = jnp.concatenate(
            [
                base + side * cores + lane
                for side in (zl, zls - 1 - zl)
                for lane in (core, cores - 1 - core)
            ]
        )
        lengths = jnp.sum(jnp.where(held[:, None] == node_ids, node_len, 0), axis=-1)
        member = jnp.any(named[None] == held[:, None, None], axis=-1)
        rank = jnp.cumsum(member.astype(jnp.int32), axis=1) - 1
        counts = jnp.sum(member.astype(jnp.int32), axis=1)
        slot_ids = lax.iota(jnp.int32, SLOTS)
        hit = member[:, None, :] & (rank[:, None, :] == slot_ids[None, :, None])
        request_ids = lax.iota(jnp.int32, requests)
        index = jnp.sum(jnp.where(hit, request_ids, 0), axis=-1)
        index = jnp.where(slot_ids[None, :] < counts[:, None], index, requests)
        smem = pl.BlockSpec(memory_space=pltpu.SMEM)
        vmem = pl.BlockSpec(memory_space=pltpu.VMEM)
        scratch = pltpu.VMEM(((requests + 1) * GROUP, HEAD_SIZE), jnp.float32)
        sent = pl.pallas_call(
            prefix_kernel,
            out_shape=jax.ShapeDtypeStruct((requests, PAD_WIDTH), jnp.float32),
            in_specs=[smem] * 4 + [vmem] * 8,
            out_specs=vmem,
            scratch_shapes=[scratch] * 4,
            compiler_params=pltpu.CompilerParams(vmem_limit_bytes=40 * 1024 * 1024),
            name="prefix_attention",
        )(
            index, counts, lengths, zh[None],
            received, cache_a, cache_b, cache_c, cache_d, own_out, own_high, own_sum,
        )
    with jax.named_scope("send_parts"):
        parts = lax.all_to_all(
            sent.reshape(zhs * kvs, rows_each, PAD_WIDTH),
            ("zh", "kv"), split_axis=0, concat_axis=0, tiled=True,
        ).reshape(zhs, kvs, rows_each, PAD_WIDTH)
    with jax.named_scope("combine"):
        return pl.pallas_call(
            final_kernel,
            out_shape=jax.ShapeDtypeStruct((rows_each, kvs * WIDTH), jnp.bfloat16),
            compiler_params=pltpu.CompilerParams(vmem_limit_bytes=32 * 1024 * 1024),
            name="combine_parts",
        )(parts)


def solution(mesh):
    owners, kvs = mesh.devices.shape
    split = Mesh(mesh.devices.reshape(4, 4, 2, 2, kvs), AXES)
    return jax.shard_map(
        shards,
        mesh=split,
        in_specs=(
            P(AXES, None),
            P(OWNER, None),
            P(),
            P(),
            P(OWNER),
            P(OWNER, None, None, "kv"),
            P(OWNER, None, None, "kv"),
            P(OWNER, None, "kv"),
        ),
        out_specs=P(AXES, None),
        check_vma=False,
    )
```

```python
import jax
import jax.numpy as jnp
from jax import lax
from jax.experimental import pallas as pl
from jax.experimental.pallas import tpu as pltpu
from jax.sharding import Mesh
from jax.sharding import PartitionSpec as P

QUERY_HEADS = 64
KEY_VALUE_HEADS = 8
HEAD_SIZE = 128
PATH = 3
GROUP = QUERY_HEADS // KEY_VALUE_HEADS
WIDTH = GROUP * HEAD_SIZE
PAD_WIDTH = WIDTH + 128
SCALE = HEAD_SIZE ** (-0.5)
LOW = -1e30
EMPTY = -(2.0**20)
TILE = 16
LANES = 128
SPREAD = 80.0
AXES = ("x", "z", "core", "kv")
OWNER = ("x", "z", "core")


def nt(a, b):
    return lax.dot_general(a, b, (((1,), (1,)), ((), ())), preferred_element_type=jnp.float32)


def nn(a, b):
    return jnp.dot(a, b, preferred_element_type=jnp.float32)


def nearest(values, unit):
    return jnp.floor(values * (1.0 / unit) + 0.5) * unit


def make_plan(held_ref, named, plan_ref):
    requests = named.shape[0]
    nodes = held_ref.shape[0]
    lanes = lax.broadcasted_iota(jnp.int32, (1, LANES), 1)
    held = jnp.full((1, LANES), -1.0, jnp.float32)
    for node in range(nodes):
        held = jnp.where(lanes == node, held_ref[node].astype(jnp.float32), held)
    member = named[:, 0:1] == held
    for step in range(1, PATH):
        member = member | (named[:, step : step + 1] == held)
    member = member.astype(jnp.float32)
    row = lax.broadcasted_iota(jnp.int32, (requests, requests), 0)
    column = lax.broadcasted_iota(jnp.int32, (requests, requests), 1)
    earlier = (column < row).astype(jnp.float32).astype(jnp.bfloat16)
    rank = nn(earlier, member.astype(jnp.bfloat16))
    rank = jnp.where(member > 0, rank, -1.0)
    counts = jnp.sum(member, axis=0, keepdims=True)
    request_ids = lax.broadcasted_iota(jnp.int32, (8, requests), 1)
    request_ids = request_ids.astype(jnp.float32).astype(jnp.bfloat16)
    slots = lanes.astype(jnp.float32)
    for node in range(nodes):
        hit = (rank[:, node : node + 1] == slots).astype(jnp.float32).astype(jnp.bfloat16)
        index = nn(request_ids, hit)[0:1]
        count = counts[:, node : node + 1]
        index = jnp.where(slots < count, index, float(requests))
        index = jnp.where(lanes == LANES - 1, count, index)
        plan_ref[node : node + 1, :] = index.astype(jnp.int32)


def suffix_part(base, cache_ref, fresh_ref, valid_ref, heads_ref, acc, high, total):
    requests, _, length, _ = cache_ref.shape
    block = 8
    rows = block * GROUP
    row_request = lax.broadcasted_iota(jnp.int32, (rows, 1), 0) // GROUP
    key_request = lax.broadcasted_iota(jnp.int32, (1, block * length), 1) // length
    fresh_request = lax.broadcasted_iota(jnp.int32, (1, requests), 1)
    own_key = row_request == key_request
    for group in range(requests // block):
        here = pl.ds(pl.multiple_of(base + group * rows, rows), rows)
        query = heads_ref[here, :].astype(jnp.bfloat16)
        keys = cache_ref[group * block : (group + 1) * block, 0].reshape(block * length, HEAD_SIZE)
        values = cache_ref[group * block : (group + 1) * block, 1].reshape(block * length, HEAD_SIZE)
        usable = own_key & (valid_ref[group : group + 1, :] > 0)
        scores = jnp.where(usable, nt(query, keys) * SCALE, LOW)
        newest = jnp.where(
            fresh_request == row_request + group * block, nt(query, fresh_ref[0]) * SCALE, LOW
        )
        top = jnp.maximum(
            jnp.max(scores, axis=1, keepdims=True), jnp.max(newest, axis=1, keepdims=True)
        )
        weights = jnp.exp(scores - top)
        newest_weights = jnp.exp(newest - top)
        part_sum = jnp.sum(weights, axis=1, keepdims=True) + jnp.sum(
            newest_weights, axis=1, keepdims=True
        )
        acc[here, :] = nn(weights.astype(jnp.bfloat16), values) + nn(
            newest_weights.astype(jnp.bfloat16), fresh_ref[1]
        )
        high[here, :] = jnp.broadcast_to(top, (rows, HEAD_SIZE))
        total[here, :] = jnp.broadcast_to(part_sum, (rows, HEAD_SIZE))


def prefix_part(first, plan_ref, length_ref, cache_ref, heads_ref, acc, high, total):
    nodes, _, longest, _ = cache_ref.shape

    def one_node(node, carry):
        place = first + node
        length = length_ref[place]
        tiles = (plan_ref[place, LANES - 1] + TILE - 1) // TILE

        def tile_of(tokens):
            valid = lax.broadcasted_iota(jnp.int32, (1, tokens), 1) < length

            def one_tile(tile, inner):
                where = [
                    pl.multiple_of(plan_ref[place, tile * TILE + slot] * GROUP, GROUP)
                    for slot in range(TILE)
                ]
                query = jnp.concatenate(
                    [heads_ref[pl.ds(at, GROUP), :] for at in where], axis=0
                ).astype(jnp.bfloat16)
                scores = jnp.where(valid, nt(query, cache_ref[node, 0, :tokens]) * SCALE, LOW)
                part_high = jnp.max(scores, axis=1, keepdims=True)
                weights = jnp.exp(scores - part_high)
                part_sum = jnp.sum(weights, axis=1, keepdims=True)
                part_out = nn(weights.astype(jnp.bfloat16), cache_ref[node, 1, :tokens])
                old_high = jnp.concatenate([high[pl.ds(at, GROUP), :] for at in where], axis=0)
                old_sum = jnp.concatenate([total[pl.ds(at, GROUP), :] for at in where], axis=0)
                old_out = jnp.concatenate([acc[pl.ds(at, GROUP), :] for at in where], axis=0)
                new_high = jnp.maximum(old_high, part_high)
                old_factor = jnp.exp(old_high - new_high)
                part_factor = jnp.exp(part_high - new_high)
                new_sum = old_sum * old_factor + part_sum * part_factor
                new_out = old_out * old_factor + part_out * part_factor
                for slot, at in enumerate(where):
                    rows = slice(slot * GROUP, (slot + 1) * GROUP)
                    high[pl.ds(at, GROUP), :] = new_high[rows]
                    total[pl.ds(at, GROUP), :] = new_sum[rows]
                    acc[pl.ds(at, GROUP), :] = new_out[rows]
                return inner

            return one_tile

        small, middle = longest // 4, longest // 2
        for low, tokens in ((0, small), (small, middle), (middle, longest)):

            @pl.when((length > low) & (length <= tokens))
            def _():
                lax.fori_loop(0, tiles, tile_of(tokens), 0)

        return carry

    lax.fori_loop(0, nodes, one_node, 0)


def write_parts(sent_ref, acc, high, total):
    requests = sent_ref.shape[0]
    lanes = lax.broadcasted_iota(jnp.int32, (1, LANES), 1)
    highs = jnp.zeros((requests, LANES), jnp.float32)
    sums = jnp.zeros((requests, LANES), jnp.float32)
    powers = jnp.zeros((requests, LANES), jnp.float32)
    for head in range(GROUP):
        rows = pl.ds(head, requests, stride=GROUP)
        part_sum = total[rows, :]
        mean = acc[rows, :] / jnp.where(part_sum > 0, part_sum, 1.0)
        largest = jnp.max(jnp.abs(mean), axis=1, keepdims=True)
        power = jnp.ceil(jnp.log2(jnp.maximum(largest, 1e-30)))
        coded = jnp.exp(mean * (jnp.exp2(-power) * SPREAD))
        sent_ref[:, head * HEAD_SIZE : (head + 1) * HEAD_SIZE] = coded.astype(jnp.bfloat16)
        highs = jnp.where(lanes == head, high[rows, :], highs)
        sums = jnp.where(lanes == head, part_sum, sums)
        powers = jnp.where(lanes == head, power, powers)
    filled = sums > 0
    coarse = jnp.where(filled, nearest(highs, 64.0), EMPTY)
    rest = jnp.where(filled, highs - coarse + jnp.log(jnp.where(filled, sums, 1.0)), 0.0)
    middle = nearest(rest, 0.25)
    fine = nearest(rest - middle, 2.0**-10)
    last = rest - middle - fine
    stats = jnp.where(lanes < GROUP, coarse, 0.0)
    for place, piece in enumerate((middle, fine, last, powers)):
        start = (place + 1) * GROUP
        moved = pltpu.roll(piece, start, 1)
        stats = jnp.where((lanes >= start) & (lanes < start + GROUP), moved, stats)
    sent_ref[:, WIDTH:] = stats.astype(jnp.bfloat16)


def attend_kernel(
    held_ref, length_ref, place_ref,
    query_ref, suffix_ref, fresh_ref, valid_ref, near_ref, far_ref,
    sent_ref,
    heads_ref, acc, high, total, plan_ref, plan_scalars, plan_sem,
):
    requests = query_ref.shape[0]
    make_plan(held_ref, query_ref[:, WIDTH:].astype(jnp.float32), plan_ref)
    plan_copy = pltpu.make_async_copy(plan_ref, plan_scalars, plan_sem)
    plan_copy.start()
    for head in range(GROUP):
        part = query_ref[:, head * HEAD_SIZE : (head + 1) * HEAD_SIZE].astype(jnp.float32)
        heads_ref[pl.ds(head, requests, stride=GROUP), :] = part
    heads_ref[requests * GROUP :, :] = jnp.zeros((GROUP, HEAD_SIZE), jnp.float32)
    acc[...] = jnp.zeros(acc.shape, jnp.float32)
    total[...] = jnp.zeros(total.shape, jnp.float32)
    high[...] = jnp.full(high.shape, LOW, jnp.float32)
    base = place_ref[0] * (suffix_ref.shape[0] * GROUP)
    suffix_part(base, suffix_ref, fresh_ref, valid_ref, heads_ref, acc, high, total)
    plan_copy.wait()
    first = 0
    for cache_ref in (near_ref, far_ref):
        prefix_part(first, plan_scalars, length_ref, cache_ref, heads_ref, acc, high, total)
        first += cache_ref.shape[0]
    write_parts(sent_ref, acc, high, total)


def combine_kernel(parts_ref, out_ref):
    sources, heads_kv, rows, _ = parts_ref.shape
    for group in range(heads_kv):
        pieces = []
        for source in range(0, sources, 2):
            stat = jnp.concatenate(
                [parts_ref[source + i, group, :, WIDTH:].astype(jnp.float32) for i in range(2)],
                axis=0,
            )
            pieces.append([stat[:, place * GROUP : (place + 1) * GROUP] for place in range(5)])
        best = pieces[0][0]
        for coarse, *_ in pieces[1:]:
            best = jnp.maximum(best, coarse)
        best = jnp.maximum(best[:rows], best[rows:])
        best = jnp.concatenate([best, best], axis=0)
        shares = [
            jnp.exp(coarse - best + (middle + fine + last))
            for coarse, middle, fine, last, _ in pieces
        ]
        denom = shares[0]
        for share in shares[1:]:
            denom = denom + share
        denom = denom[:rows] + denom[rows:]
        denom = jnp.concatenate([denom, denom], axis=0) * SPREAD
        factors = [
            share * jnp.exp2(power) / denom for share, (*_, power) in zip(shares, pieces)
        ]
        for head in range(GROUP):
            columns = slice(head * HEAD_SIZE, (head + 1) * HEAD_SIZE)
            result = 0.0
            for pair, factor in enumerate(factors):
                coded = jnp.concatenate(
                    [
                        parts_ref[2 * pair + i, group, :, columns].astype(jnp.float32)
                        for i in range(2)
                    ],
                    axis=0,
                )
                result = result + factor[:, head : head + 1] * jnp.log(coded)
            start = group * WIDTH + head * HEAD_SIZE
            out_ref[:, start : start + HEAD_SIZE] = (result[:rows] + result[rows:]).astype(
                jnp.bfloat16
            )


def shards(
    queries, paths, node_owner, node_len, suf_len, prefix_kv, suffix_key_value, fresh_key_value
):
    x, z, core, kv = [lax.axis_index(name) for name in AXES]
    xs, zs, cores, kvs = [lax.axis_size(name) for name in AXES]
    rows_each = queries.shape[0]
    request_count = paths.shape[0]
    requests = zs * request_count
    node_ids = lax.iota(jnp.int32, node_owner.shape[0])
    smem = pl.BlockSpec(memory_space=pltpu.SMEM)
    vmem = pl.BlockSpec(memory_space=pltpu.VMEM)

    def exchange(slabs):
        return lax.all_to_all(slabs, ("z", "kv"), split_axis=0, concat_axis=0, tiled=True)

    with jax.named_scope("send_queries"):
        my_paths = lax.dynamic_slice_in_dim(paths, kv * rows_each, rows_each, 0)
        my_holders = jnp.sum(
            jnp.where(my_paths[:, :, None] == node_ids, node_owner, 0), axis=-1
        )
        tail = jnp.pad(my_holders, ((0, 0), (0, LANES - PATH))).astype(jnp.bfloat16)
        by_head = queries.reshape(rows_each, kvs, WIDTH).transpose(1, 0, 2)
        outgoing = jnp.concatenate(
            [by_head, jnp.broadcast_to(tail[None], (kvs, rows_each, LANES))], axis=-1
        )
        outgoing = jnp.broadcast_to(outgoing[None], (zs,) + outgoing.shape)
        outgoing, own_cache = lax.optimization_barrier((outgoing, prefix_kv))
    with jax.named_scope("send_prefix"):
        ring = [own_cache]
        for step in range(1, xs):
            hops = [(i, (i + step) % xs) for i in range(xs)]
            ring.append(lax.ppermute(own_cache, "x", hops))
        near = jnp.concatenate(ring, axis=0)
        far = lax.ppermute(near, "core", [(0, 1), (1, 0)])
    with jax.named_scope("send_queries"):
        received = exchange(outgoing.reshape(zs * kvs, rows_each, PAD_WIDTH))
        received = received.reshape(requests, PAD_WIDTH)
    with jax.named_scope("attend"):
        chip = (x - lax.iota(jnp.int32, xs)) % xs
        held = jnp.concatenate([(chip * zs + z) * cores + lane for lane in (core, cores - 1 - core)])
        lengths = jnp.sum(jnp.where(held[:, None] == node_ids, node_len, 0), axis=-1)
        length = suffix_key_value.shape[2]
        valid = (lax.iota(jnp.int32, length)[None, :] < suf_len[:, None]).astype(jnp.int32)
        rows = pltpu.VMEM(((requests + 1) * GROUP, HEAD_SIZE), jnp.float32)
        plan = (xs * cores, LANES)
        sent = pl.pallas_call(
            attend_kernel,
            out_shape=jax.ShapeDtypeStruct((requests, PAD_WIDTH), jnp.bfloat16),
            in_specs=[smem] * 3 + [vmem] * 6,
            out_specs=vmem,
            scratch_shapes=[rows] * 4
            + [
                pltpu.VMEM(plan, jnp.int32),
                pltpu.SMEM(plan, jnp.int32),
                pltpu.SemaphoreType.DMA,
            ],
            compiler_params=pltpu.CompilerParams(vmem_limit_bytes=40 * 1024 * 1024),
            name="attend",
        )(
            held, lengths, z[None],
            received, suffix_key_value, fresh_key_value.transpose(1, 0, 2),
            valid.reshape(-1, 8 * length), near, far,
        )
    with jax.named_scope("send_parts"):
        parts = exchange(sent.reshape(zs * kvs, rows_each, PAD_WIDTH))
        parts = parts.reshape(zs, kvs, rows_each, PAD_WIDTH)
    with jax.named_scope("combine"):
        return pl.pallas_call(
            combine_kernel,
            out_shape=jax.ShapeDtypeStruct((rows_each, kvs * WIDTH), jnp.bfloat16),
            compiler_params=pltpu.CompilerParams(vmem_limit_bytes=32 * 1024 * 1024),
            name="combine",
        )(parts)


def solution(mesh):
    owners, kvs = mesh.devices.shape
    split = Mesh(mesh.devices.reshape(4, 8, 2, kvs), AXES)
    return jax.shard_map(
        shards,
        mesh=split,
        in_specs=(
            P(AXES, None),
            P(OWNER, None),
            P(),
            P(),
            P(OWNER),
            P(OWNER, None, None, "kv"),
            P(OWNER, None, None, "kv"),
            P(OWNER, None, "kv"),
        ),
        out_specs=P(AXES, None),
        check_vma=False,
    )
```

```python
import jax
import jax.numpy as jnp
from jax import lax
from jax.experimental import pallas as pl
from jax.experimental.pallas import tpu as pltpu
from jax.sharding import Mesh
from jax.sharding import PartitionSpec as P

QUERY_HEADS = 64
KEY_VALUE_HEADS = 8
HEAD_SIZE = 128
PATH = 3
GROUP = QUERY_HEADS // KEY_VALUE_HEADS
WIDTH = GROUP * HEAD_SIZE
PAD_WIDTH = WIDTH + 128
SCALE = HEAD_SIZE ** (-0.5)
LOW = -1e30
EMPTY = -(2.0**20)
TILE = 16
LANES = 128
SPREAD = 80.0
AXES = ("x", "z", "core", "kv")
OWNER = ("x", "z", "core")
SWAPS = (0, 1, 3, 2)


def nt(a, b):
    return lax.dot_general(a, b, (((1,), (1,)), ((), ())), preferred_element_type=jnp.float32)


def nn(a, b):
    return jnp.dot(a, b, preferred_element_type=jnp.float32)


def nearest(values, unit):
    return jnp.floor(values * (1.0 / unit) + 0.5) * unit


def make_plan(held_ref, named, plan_ref):
    requests = named.shape[0]
    nodes = held_ref.shape[0]
    lanes = lax.broadcasted_iota(jnp.int32, (1, LANES), 1)
    held = jnp.full((1, LANES), -1.0, jnp.float32)
    for node in range(nodes):
        held = jnp.where(lanes == node, held_ref[node].astype(jnp.float32), held)
    member = named[:, 0:1] == held
    for step in range(1, PATH):
        member = member | (named[:, step : step + 1] == held)
    member = member.astype(jnp.float32)
    row = lax.broadcasted_iota(jnp.int32, (requests, requests), 0)
    column = lax.broadcasted_iota(jnp.int32, (requests, requests), 1)
    earlier = (column < row).astype(jnp.float32).astype(jnp.bfloat16)
    rank = nn(earlier, member.astype(jnp.bfloat16))
    rank = jnp.where(member > 0, rank, -1.0)
    counts = jnp.sum(member, axis=0, keepdims=True)
    request_ids = lax.broadcasted_iota(jnp.int32, (8, requests), 1)
    request_ids = request_ids.astype(jnp.float32).astype(jnp.bfloat16)
    slots = lanes.astype(jnp.float32)
    for node in range(nodes):
        hit = (rank[:, node : node + 1] == slots).astype(jnp.float32).astype(jnp.bfloat16)
        index = nn(request_ids, hit)[0:1]
        count = counts[:, node : node + 1]
        index = jnp.where(slots < count, index, float(requests))
        index = jnp.where(lanes == LANES - 1, count, index)
        plan_ref[node : node + 1, :] = index.astype(jnp.int32)


def suffix_part(base, cache_ref, fresh_ref, valid_ref, heads_ref, acc, high, total):
    requests, _, length, _ = cache_ref.shape
    block = 8
    rows = block * GROUP
    row_request = lax.broadcasted_iota(jnp.int32, (rows, 1), 0) // GROUP
    key_request = lax.broadcasted_iota(jnp.int32, (1, block * length), 1) // length
    fresh_request = lax.broadcasted_iota(jnp.int32, (1, requests), 1)
    own_key = row_request == key_request
    for group in range(requests // block):
        here = pl.ds(pl.multiple_of(base + group * rows, rows), rows)
        query = heads_ref[here, :].astype(jnp.bfloat16)
        keys = cache_ref[group * block : (group + 1) * block, 0].reshape(block * length, HEAD_SIZE)
        values = cache_ref[group * block : (group + 1) * block, 1].reshape(block * length, HEAD_SIZE)
        usable = own_key & (valid_ref[group : group + 1, :] > 0)
        scores = jnp.where(usable, nt(query, keys) * SCALE, LOW)
        newest = jnp.where(
            fresh_request == row_request + group * block, nt(query, fresh_ref[0]) * SCALE, LOW
        )
        top = jnp.maximum(
            jnp.max(scores, axis=1, keepdims=True), jnp.max(newest, axis=1, keepdims=True)
        )
        weights = jnp.exp(scores - top)
        newest_weights = jnp.exp(newest - top)
        part_sum = jnp.sum(weights, axis=1, keepdims=True) + jnp.sum(
            newest_weights, axis=1, keepdims=True
        )
        acc[here, :] = nn(weights.astype(jnp.bfloat16), values) + nn(
            newest_weights.astype(jnp.bfloat16), fresh_ref[1]
        )
        high[here, :] = jnp.broadcast_to(top, (rows, HEAD_SIZE))
        total[here, :] = jnp.broadcast_to(part_sum, (rows, HEAD_SIZE))


def prefix_part(plan_ref, length_ref, near_ref, far_ref, heads_ref, acc, high, total):
    nodes, _, longest, _ = near_ref.shape

    def one_pair(node, carry):
        places = (node, node + nodes)
        lengths = [length_ref[place] for place in places]
        most = jnp.maximum(lengths[0], lengths[1])
        count = jnp.maximum(plan_ref[places[0], LANES - 1], plan_ref[places[1], LANES - 1])
        tiles = (count + TILE - 1) // TILE

        def tile_of(tokens):
            columns = lax.broadcasted_iota(jnp.int32, (1, tokens), 1)
            masks = [columns < length for length in lengths]

            def one_tile(tile, inner):
                where = [
                    [
                        pl.multiple_of(plan_ref[place, tile * TILE + slot] * GROUP, GROUP)
                        for slot in range(TILE)
                    ]
                    for place in places
                ]
                parts = []
                for spots, mask, cache_ref in zip(where, masks, (near_ref, far_ref)):
                    query = jnp.concatenate(
                        [heads_ref[pl.ds(at, GROUP), :] for at in spots], axis=0
                    ).astype(jnp.bfloat16)
                    scores = jnp.where(mask, nt(query, cache_ref[node, 0, :tokens]) * SCALE, LOW)
                    part_high = jnp.max(scores, axis=1, keepdims=True)
                    weights = jnp.exp(scores - part_high)
                    part_sum = jnp.sum(weights, axis=1, keepdims=True)
                    part_out = nn(weights.astype(jnp.bfloat16), cache_ref[node, 1, :tokens])
                    parts.append((part_high, part_sum, part_out))
                for spots, (part_high, part_sum, part_out) in zip(where, parts):
                    old_high = jnp.concatenate([high[pl.ds(at, GROUP), :] for at in spots], axis=0)
                    old_sum = jnp.concatenate([total[pl.ds(at, GROUP), :] for at in spots], axis=0)
                    old_out = jnp.concatenate([acc[pl.ds(at, GROUP), :] for at in spots], axis=0)
                    new_high = jnp.maximum(old_high, part_high)
                    old_factor = jnp.exp(old_high - new_high)
                    part_factor = jnp.exp(part_high - new_high)
                    new_sum = old_sum * old_factor + part_sum * part_factor
                    new_out = old_out * old_factor + part_out * part_factor
                    for slot, at in enumerate(spots):
                        rows = slice(slot * GROUP, (slot + 1) * GROUP)
                        high[pl.ds(at, GROUP), :] = new_high[rows]
                        total[pl.ds(at, GROUP), :] = new_sum[rows]
                        acc[pl.ds(at, GROUP), :] = new_out[rows]
                return inner

            return one_tile

        small, middle = longest // 4, longest // 2
        for low, tokens in ((0, small), (small, middle), (middle, longest)):

            @pl.when((most > low) & (most <= tokens))
            def _():
                lax.fori_loop(0, tiles, tile_of(tokens), 0)

        return carry

    lax.fori_loop(0, nodes, one_pair, 0)


def write_parts(sent_ref, acc, high, total):
    requests = sent_ref.shape[0]
    lanes = lax.broadcasted_iota(jnp.int32, (1, LANES), 1)
    highs = jnp.zeros((requests, LANES), jnp.float32)
    sums = jnp.zeros((requests, LANES), jnp.float32)
    tops = jnp.zeros((requests, LANES), jnp.float32)
    for head in range(GROUP):
        rows = pl.ds(head, requests, stride=GROUP)
        top = jnp.max(jnp.abs(acc[rows, :]), axis=1, keepdims=True)
        highs = jnp.where(lanes == head, high[rows, :], highs)
        sums = jnp.where(lanes == head, total[rows, :], sums)
        tops = jnp.where(lanes == head, top, tops)
    share = 1.0 / jnp.where(sums > 0, sums, 1.0)
    powers = jnp.ceil(jnp.log2(jnp.maximum(tops * share, 1e-30)))
    factors = share * (jnp.exp2(-powers) * SPREAD)
    for head in range(GROUP):
        rows = pl.ds(head, requests, stride=GROUP)
        coded = jnp.exp(acc[rows, :] * factors[:, head : head + 1])
        sent_ref[:, head * HEAD_SIZE : (head + 1) * HEAD_SIZE] = coded.astype(jnp.bfloat16)
    filled = sums > 0
    coarse = jnp.where(filled, nearest(highs, 64.0), EMPTY)
    rest = jnp.where(filled, highs - coarse + jnp.log(jnp.where(filled, sums, 1.0)), 0.0)
    middle = nearest(rest, 0.25)
    fine = nearest(rest - middle, 2.0**-10)
    last = rest - middle - fine
    stats = jnp.where(lanes < GROUP, coarse, 0.0)
    for place, piece in enumerate((middle, fine, last, powers)):
        start = (place + 1) * GROUP
        moved = pltpu.roll(piece, start, 1)
        stats = jnp.where((lanes >= start) & (lanes < start + GROUP), moved, stats)
    sent_ref[:, WIDTH:] = stats.astype(jnp.bfloat16)


def pack_kernel(place_ref, paths_ref, owner_ref, query_ref, sent_ref):
    heads_kv = KEY_VALUE_HEADS
    copies = sent_ref.shape[0] // heads_kv
    rows = query_ref.shape[0]
    lanes = lax.broadcasted_iota(jnp.int32, (rows, LANES), 1)
    sublanes = lax.broadcasted_iota(jnp.int32, (rows, LANES), 0)
    tail = jnp.zeros((rows, LANES), jnp.float32)
    for row in range(rows):
        for step in range(PATH):
            node = paths_ref[step, place_ref[0] * rows + row]
            holder = owner_ref[node].astype(jnp.float32)
            tail = jnp.where((sublanes == row) & (lanes == step), holder, tail)
    tail = tail.astype(jnp.bfloat16)
    for group in range(heads_kv):
        part = query_ref[:, group * WIDTH : (group + 1) * WIDTH]
        for copy in range(copies):
            sent_ref[copy * heads_kv + group, :, :WIDTH] = part
            sent_ref[copy * heads_kv + group, :, WIDTH:] = tail


def local_kernel(
    held_ref, query_ref, own_ref, fresh_ref, valid_ref, stored_ref,
    plan_ref, heads_ref, acc, high, total,
    own_heads_ref, suffix_ref, suffix_sem,
):
    fetch = pltpu.make_async_copy(stored_ref, suffix_ref, suffix_sem)
    fetch.start()
    requests = query_ref.shape[0]
    make_plan(held_ref, query_ref[:, WIDTH:].astype(jnp.float32), plan_ref)
    for head in range(GROUP):
        columns = slice(head * HEAD_SIZE, (head + 1) * HEAD_SIZE)
        part = query_ref[:, columns].astype(jnp.float32)
        heads_ref[pl.ds(head, requests, stride=GROUP), :] = part
        part = own_ref[:, columns].astype(jnp.float32)
        own_heads_ref[pl.ds(head, own_ref.shape[0], stride=GROUP), :] = part
    heads_ref[requests * GROUP :, :] = jnp.zeros((GROUP, HEAD_SIZE), jnp.float32)
    fetch.wait()
    suffix_part(0, suffix_ref, fresh_ref, valid_ref, own_heads_ref, acc, high, total)


def prefix_kernel(
    plan_ref, length_ref, place_ref,
    heads_ref, own_out, own_high, own_sum, near_ref, far_ref,
    sent_ref,
    acc, high, total, near_cache, far_cache, near_sem, far_sem,
):
    near_fetch = pltpu.make_async_copy(near_ref, near_cache, near_sem)
    far_fetch = pltpu.make_async_copy(far_ref, far_cache, far_sem)
    near_fetch.start()
    far_fetch.start()
    acc[...] = jnp.zeros(acc.shape, jnp.float32)
    total[...] = jnp.zeros(total.shape, jnp.float32)
    high[...] = jnp.full(high.shape, LOW, jnp.float32)
    own_rows = own_out.shape[0]
    own = pl.ds(pl.multiple_of(place_ref[0] * own_rows, own_rows), own_rows)
    acc[own, :] = own_out[...]
    high[own, :] = own_high[...]
    total[own, :] = own_sum[...]
    near_fetch.wait()
    far_fetch.wait()
    prefix_part(plan_ref, length_ref, near_cache, far_cache, heads_ref, acc, high, total)
    write_parts(sent_ref, acc, high, total)


def combine_kernel(parts_ref, out_ref):
    sources, heads_kv, rows, _ = parts_ref.shape
    for group in range(heads_kv):
        pieces = []
        for source in range(0, sources, 2):
            stat = jnp.concatenate(
                [parts_ref[source + i, group, :, WIDTH:].astype(jnp.float32) for i in range(2)],
                axis=0,
            )
            pieces.append([stat[:, place * GROUP : (place + 1) * GROUP] for place in range(5)])
        best = pieces[0][0]
        for coarse, *_ in pieces[1:]:
            best = jnp.maximum(best, coarse)
        best = jnp.maximum(best[:rows], best[rows:])
        best = jnp.concatenate([best, best], axis=0)
        shares = [
            jnp.exp(coarse - best + (middle + fine + last))
            for coarse, middle, fine, last, _ in pieces
        ]
        denom = shares[0]
        for share in shares[1:]:
            denom = denom + share
        denom = denom[:rows] + denom[rows:]
        denom = jnp.concatenate([denom, denom], axis=0) * SPREAD
        factors = [
            share * jnp.exp2(power) / denom for share, (*_, power) in zip(shares, pieces)
        ]
        for head in range(GROUP):
            columns = slice(head * HEAD_SIZE, (head + 1) * HEAD_SIZE)
            result = 0.0
            for pair, factor in enumerate(factors):
                coded = jnp.concatenate(
                    [
                        parts_ref[2 * pair + i, group, :, columns].astype(jnp.float32)
                        for i in range(2)
                    ],
                    axis=0,
                )
                result = result + factor[:, head : head + 1] * jnp.log(coded)
            start = group * WIDTH + head * HEAD_SIZE
            out_ref[:, start : start + HEAD_SIZE] = (result[:rows] + result[rows:]).astype(
                jnp.bfloat16
            )


def shards(
    queries, paths, node_owner, node_len, suf_len, prefix_kv, suffix_key_value, fresh_key_value
):
    x, z, core, kv = [lax.axis_index(name) for name in AXES]
    xs, zs, cores, kvs = [lax.axis_size(name) for name in AXES]
    rows_each = queries.shape[0]
    request_count = paths.shape[0]
    requests = zs * request_count
    smem = pl.BlockSpec(memory_space=pltpu.SMEM)
    vmem = pl.BlockSpec(memory_space=pltpu.VMEM)
    anywhere = pl.BlockSpec(memory_space=pl.ANY)
    hbm = pl.BlockSpec(memory_space=pltpu.HBM)

    def exchange(slabs):
        return lax.all_to_all(slabs, ("z", "kv"), split_axis=0, concat_axis=0, tiled=True)

    with jax.named_scope("send_queries"):
        outgoing = pl.pallas_call(
            pack_kernel,
            out_shape=jax.ShapeDtypeStruct((zs * kvs, rows_each, PAD_WIDTH), jnp.bfloat16),
            in_specs=[smem] * 3 + [vmem],
            out_specs=vmem,
            name="pack_queries",
        )(kv[None], paths.T, node_owner, queries)
        outgoing, own_cache = lax.optimization_barrier((outgoing, prefix_kv))
    with jax.named_scope("send_prefix"):
        ring = [own_cache]
        for step in SWAPS[1:]:
            ring.append(lax.ppermute(own_cache, "x", [(i, i ^ step) for i in range(xs)]))
        near = jnp.concatenate(ring, axis=0)
        far = lax.ppermute(near, "core", [(0, 1), (1, 0)])
    with jax.named_scope("send_queries"):
        received = exchange(outgoing)
        received = received.reshape(requests, PAD_WIDTH)
    with jax.named_scope("attend"):
        node_ids = lax.iota(jnp.int32, node_len.shape[0])
        chip = x ^ jnp.array(SWAPS, jnp.int32)
        held = jnp.concatenate([(chip * zs + z) * cores + lane for lane in (core, cores - 1 - core)])
        lengths = jnp.sum(jnp.where(held[:, None] == node_ids, node_len, 0), axis=-1)
        length = suffix_key_value.shape[2]
        valid = (lax.iota(jnp.int32, length)[None, :] < suf_len[:, None]).astype(jnp.int32)
        all_rows = ((requests + 1) * GROUP, HEAD_SIZE)
        own_rows = (request_count * GROUP, HEAD_SIZE)
        own = lax.dynamic_slice_in_dim(received, z * request_count, request_count, 0)
        own_part = jax.ShapeDtypeStruct(own_rows, jnp.float32)
        plan, heads, *own_parts = pl.pallas_call(
            local_kernel,
            out_shape=(
                jax.ShapeDtypeStruct((xs * cores, LANES), jnp.int32),
                jax.ShapeDtypeStruct(all_rows, jnp.float32),
                own_part, own_part, own_part,
            ),
            in_specs=[smem] + [vmem] * 4 + [hbm],
            out_specs=[vmem] * 5,
            scratch_shapes=[
                pltpu.VMEM(own_rows, jnp.float32),
                pltpu.VMEM(suffix_key_value.shape, jnp.bfloat16),
                pltpu.SemaphoreType.DMA,
            ],
            compiler_params=pltpu.CompilerParams(vmem_limit_bytes=32 * 1024 * 1024),
            cost_estimate=pl.CostEstimate(flops=17179869184, bytes_accessed=67108864, transcendentals=1 << 20),
            name="local_attention",
        )(
            held, received, own, fresh_key_value.transpose(1, 0, 2),
            valid.reshape(-1, 8 * length), suffix_key_value,
        )
        sent = pl.pallas_call(
            prefix_kernel,
            out_shape=jax.ShapeDtypeStruct((requests, PAD_WIDTH), jnp.bfloat16),
            in_specs=[smem] * 3 + [vmem] * 4 + [anywhere] * 2,
            out_specs=vmem,
            scratch_shapes=[pltpu.VMEM(all_rows, jnp.float32)] * 3
            + [pltpu.VMEM(near.shape, jnp.bfloat16)] * 2
            + [pltpu.SemaphoreType.DMA] * 2,
            compiler_params=pltpu.CompilerParams(vmem_limit_bytes=40 * 1024 * 1024),
            name="prefix_attention",
        )(plan, lengths, z[None], heads, *own_parts, near, far)
    with jax.named_scope("send_parts"):
        parts = exchange(sent.reshape(zs * kvs, rows_each, PAD_WIDTH))
        parts = parts.reshape(zs, kvs, rows_each, PAD_WIDTH)
    with jax.named_scope("combine"):
        return pl.pallas_call(
            combine_kernel,
            out_shape=jax.ShapeDtypeStruct((rows_each, kvs * WIDTH), jnp.bfloat16),
            compiler_params=pltpu.CompilerParams(vmem_limit_bytes=32 * 1024 * 1024),
            name="combine",
        )(parts)


def solution(mesh):
    owners, kvs = mesh.devices.shape
    split = Mesh(mesh.devices.reshape(4, 8, 2, kvs), AXES)
    return jax.shard_map(
        shards,
        mesh=split,
        in_specs=(
            P(AXES, None),
            P(OWNER, None),
            P(),
            P(),
            P(OWNER),
            P(OWNER, None, None, "kv"),
            P(OWNER, None, None, "kv"),
            P(OWNER, None, "kv"),
        ),
        out_specs=P(AXES, None),
        check_vma=False,
    )
```

```python
import jax
import jax.numpy as jnp
from jax import lax
from jax.experimental import pallas as pl
from jax.experimental.pallas import tpu as pltpu
from jax.sharding import Mesh
from jax.sharding import PartitionSpec as P

QUERY_HEADS = 64
KEY_VALUE_HEADS = 8
HEAD_SIZE = 128
PATH = 3
GROUP = QUERY_HEADS // KEY_VALUE_HEADS
WIDTH = GROUP * HEAD_SIZE
PAD_WIDTH = WIDTH + 128
SCALE = HEAD_SIZE ** (-0.5)
LOW = -1e30
EMPTY = -(2.0**20)
TILE = 16
LANES = 128
SPREAD = 80.0
AXES = ("x", "z", "core", "kv")
OWNER = ("x", "z", "core")
SWAPS = (0, 1, 3, 2)


def nt(a, b):
    return lax.dot_general(a, b, (((1,), (1,)), ((), ())), preferred_element_type=jnp.float32)


def nn(a, b):
    return jnp.dot(a, b, preferred_element_type=jnp.float32)


def nearest(values, unit):
    return jnp.floor(values * (1.0 / unit) + 0.5) * unit


def make_plan(held_ref, named, plan_ref):
    requests = named.shape[0]
    nodes = held_ref.shape[0]
    lanes = lax.broadcasted_iota(jnp.int32, (1, LANES), 1)
    held = jnp.full((1, LANES), -1.0, jnp.float32)
    for node in range(nodes):
        held = jnp.where(lanes == node, held_ref[node].astype(jnp.float32), held)
    member = named[:, 0:1] == held
    for step in range(1, PATH):
        member = member | (named[:, step : step + 1] == held)
    member = member.astype(jnp.float32)
    row = lax.broadcasted_iota(jnp.int32, (requests, requests), 0)
    column = lax.broadcasted_iota(jnp.int32, (requests, requests), 1)
    earlier = (column < row).astype(jnp.float32).astype(jnp.bfloat16)
    rank = nn(earlier, member.astype(jnp.bfloat16))
    rank = jnp.where(member > 0, rank, -1.0)
    counts = jnp.sum(member, axis=0, keepdims=True)
    request_ids = lax.broadcasted_iota(jnp.int32, (8, requests), 1)
    request_ids = request_ids.astype(jnp.float32).astype(jnp.bfloat16)
    slots = lanes.astype(jnp.float32)
    for node in range(nodes):
        hit = (rank[:, node : node + 1] == slots).astype(jnp.float32).astype(jnp.bfloat16)
        index = nn(request_ids, hit)[0:1]
        count = counts[:, node : node + 1]
        index = jnp.where(slots < count, index, float(requests))
        index = jnp.where(lanes == LANES - 1, count, index)
        plan_ref[node : node + 1, :] = index.astype(jnp.int32)


def suffix_part(base, cache_ref, fresh_ref, valid_ref, heads_ref, acc, high, total):
    requests, _, length, _ = cache_ref.shape
    block = 8
    rows = block * GROUP
    row_request = lax.broadcasted_iota(jnp.int32, (rows, 1), 0) // GROUP
    key_request = lax.broadcasted_iota(jnp.int32, (1, block * length), 1) // length
    fresh_request = lax.broadcasted_iota(jnp.int32, (1, requests), 1)
    own_key = row_request == key_request
    for group in range(requests // block):
        here = pl.ds(pl.multiple_of(base + group * rows, rows), rows)
        query = heads_ref[here, :].astype(jnp.bfloat16)
        keys = cache_ref[group * block : (group + 1) * block, 0].reshape(block * length, HEAD_SIZE)
        values = cache_ref[group * block : (group + 1) * block, 1].reshape(block * length, HEAD_SIZE)
        usable = own_key & (valid_ref[group : group + 1, :] > 0)
        scores = jnp.where(usable, nt(query, keys) * SCALE, LOW)
        newest = jnp.where(
            fresh_request == row_request + group * block, nt(query, fresh_ref[0]) * SCALE, LOW
        )
        top = jnp.maximum(
            jnp.max(scores, axis=1, keepdims=True), jnp.max(newest, axis=1, keepdims=True)
        )
        weights = jnp.exp(scores - top)
        newest_weights = jnp.exp(newest - top)
        part_sum = jnp.sum(weights, axis=1, keepdims=True) + jnp.sum(
            newest_weights, axis=1, keepdims=True
        )
        acc[here, :] = nn(weights.astype(jnp.bfloat16), values) + nn(
            newest_weights.astype(jnp.bfloat16), fresh_ref[1]
        )
        high[here, :] = jnp.broadcast_to(top, (rows, HEAD_SIZE))
        total[here, :] = jnp.broadcast_to(part_sum, (rows, HEAD_SIZE))


def prefix_part(plan_ref, length_ref, near_ref, far_ref, heads_ref, acc, high, total):
    nodes, _, longest, _ = near_ref.shape

    def one_pair(node, carry):
        places = (node, node + nodes)
        lengths = [length_ref[place] for place in places]
        most = jnp.maximum(lengths[0], lengths[1])
        count = jnp.maximum(plan_ref[places[0], LANES - 1], plan_ref[places[1], LANES - 1])
        tiles = (count + TILE - 1) // TILE

        def tile_of(tokens):
            columns = lax.broadcasted_iota(jnp.int32, (1, tokens), 1)
            masks = [columns < length for length in lengths]

            def one_tile(tile, inner):
                where = [
                    [
                        pl.multiple_of(plan_ref[place, tile * TILE + slot] * GROUP, GROUP)
                        for slot in range(TILE)
                    ]
                    for place in places
                ]
                parts = []
                for spots, mask, cache_ref in zip(where, masks, (near_ref, far_ref)):
                    query = jnp.concatenate(
                        [heads_ref[pl.ds(at, GROUP), :] for at in spots], axis=0
                    ).astype(jnp.bfloat16)
                    scores = jnp.where(mask, nt(query, cache_ref[node, 0, :tokens]) * SCALE, LOW)
                    part_high = jnp.max(scores, axis=1, keepdims=True)
                    weights = jnp.exp(scores - part_high)
                    part_sum = jnp.sum(weights, axis=1, keepdims=True)
                    part_out = nn(weights.astype(jnp.bfloat16), cache_ref[node, 1, :tokens])
                    parts.append((part_high, part_sum, part_out))
                for spots, (part_high, part_sum, part_out) in zip(where, parts):
                    old_high = jnp.concatenate([high[pl.ds(at, GROUP), :] for at in spots], axis=0)
                    old_sum = jnp.concatenate([total[pl.ds(at, GROUP), :] for at in spots], axis=0)
                    old_out = jnp.concatenate([acc[pl.ds(at, GROUP), :] for at in spots], axis=0)
                    new_high = jnp.maximum(old_high, part_high)
                    old_factor = jnp.exp(old_high - new_high)
                    part_factor = jnp.exp(part_high - new_high)
                    new_sum = old_sum * old_factor + part_sum * part_factor
                    new_out = old_out * old_factor + part_out * part_factor
                    for slot, at in enumerate(spots):
                        rows = slice(slot * GROUP, (slot + 1) * GROUP)
                        high[pl.ds(at, GROUP), :] = new_high[rows]
                        total[pl.ds(at, GROUP), :] = new_sum[rows]
                        acc[pl.ds(at, GROUP), :] = new_out[rows]
                return inner

            return one_tile

        small, middle = longest // 4, longest // 2
        for low, tokens in ((0, small), (small, middle), (middle, longest)):

            @pl.when((most > low) & (most <= tokens))
            def _():
                lax.fori_loop(0, tiles, tile_of(tokens), 0)

        return carry

    lax.fori_loop(0, nodes, one_pair, 0)


def write_parts(sent_ref, acc, high, total):
    requests = sent_ref.shape[0]
    lanes = lax.broadcasted_iota(jnp.int32, (1, LANES), 1)
    highs = jnp.zeros((requests, LANES), jnp.float32)
    sums = jnp.zeros((requests, LANES), jnp.float32)
    tops = jnp.zeros((requests, LANES), jnp.float32)
    for head in range(GROUP):
        rows = pl.ds(head, requests, stride=GROUP)
        top = jnp.max(jnp.abs(acc[rows, :]), axis=1, keepdims=True)
        highs = jnp.where(lanes == head, high[rows, :], highs)
        sums = jnp.where(lanes == head, total[rows, :], sums)
        tops = jnp.where(lanes == head, top, tops)
    share = 1.0 / jnp.where(sums > 0, sums, 1.0)
    powers = jnp.ceil(jnp.log2(jnp.maximum(tops * share, 1e-30)))
    factors = share * (jnp.exp2(-powers) * SPREAD)
    for head in range(GROUP):
        rows = pl.ds(head, requests, stride=GROUP)
        coded = jnp.exp(acc[rows, :] * factors[:, head : head + 1])
        sent_ref[:, head * HEAD_SIZE : (head + 1) * HEAD_SIZE] = coded.astype(jnp.bfloat16)
    filled = sums > 0
    coarse = jnp.where(filled, nearest(highs, 64.0), EMPTY)
    rest = jnp.where(filled, highs - coarse + jnp.log(jnp.where(filled, sums, 1.0)), 0.0)
    middle = nearest(rest, 0.25)
    fine = nearest(rest - middle, 2.0**-10)
    last = rest - middle - fine
    stats = jnp.where(lanes < GROUP, coarse, 0.0)
    for place, piece in enumerate((middle, fine, last, powers)):
        start = (place + 1) * GROUP
        moved = pltpu.roll(piece, start, 1)
        stats = jnp.where((lanes >= start) & (lanes < start + GROUP), moved, stats)
    sent_ref[:, WIDTH:] = stats.astype(jnp.bfloat16)


def pack_kernel(place_ref, paths_ref, owner_ref, query_ref, sent_ref):
    heads_kv = KEY_VALUE_HEADS
    copies = sent_ref.shape[0] // heads_kv
    rows = query_ref.shape[0]
    lanes = lax.broadcasted_iota(jnp.int32, (rows, LANES), 1)
    sublanes = lax.broadcasted_iota(jnp.int32, (rows, LANES), 0)
    tail = jnp.zeros((rows, LANES), jnp.float32)
    for row in range(rows):
        for step in range(PATH):
            node = paths_ref[step, place_ref[0] * rows + row]
            holder = owner_ref[node].astype(jnp.float32)
            tail = jnp.where((sublanes == row) & (lanes == step), holder, tail)
    tail = tail.astype(jnp.bfloat16)
    for group in range(heads_kv):
        part = query_ref[:, group * WIDTH : (group + 1) * WIDTH]
        for copy in range(copies):
            sent_ref[copy * heads_kv + group, :, :WIDTH] = part
            sent_ref[copy * heads_kv + group, :, WIDTH:] = tail


def plan_kernel(held_ref, query_ref, plan_ref, heads_ref):
    requests = query_ref.shape[0]
    make_plan(held_ref, query_ref[:, WIDTH:].astype(jnp.float32), plan_ref)
    for head in range(GROUP):
        part = query_ref[:, head * HEAD_SIZE : (head + 1) * HEAD_SIZE].astype(jnp.float32)
        heads_ref[pl.ds(head, requests, stride=GROUP), :] = part
    heads_ref[requests * GROUP :, :] = jnp.zeros((GROUP, HEAD_SIZE), jnp.float32)


def local_kernel(
    own_ref, fresh_ref, valid_ref, suffix_ref, acc, high, total, own_heads_ref
):
    for head in range(GROUP):
        part = own_ref[:, head * HEAD_SIZE : (head + 1) * HEAD_SIZE].astype(jnp.float32)
        own_heads_ref[pl.ds(head, own_ref.shape[0], stride=GROUP), :] = part
    suffix_part(0, suffix_ref, fresh_ref, valid_ref, own_heads_ref, acc, high, total)


def prefix_kernel(
    plan_ref, length_ref, place_ref,
    heads_ref, own_out, own_high, own_sum, near_ref, far_ref,
    sent_ref,
    acc, high, total, near_cache, far_cache, near_sem, far_sem,
):
    near_fetch = pltpu.make_async_copy(near_ref, near_cache, near_sem)
    far_fetch = pltpu.make_async_copy(far_ref, far_cache, far_sem)
    near_fetch.start()
    far_fetch.start()
    acc[...] = jnp.zeros(acc.shape, jnp.float32)
    total[...] = jnp.zeros(total.shape, jnp.float32)
    high[...] = jnp.full(high.shape, LOW, jnp.float32)
    own_rows = own_out.shape[0]
    own = pl.ds(pl.multiple_of(place_ref[0] * own_rows, own_rows), own_rows)
    acc[own, :] = own_out[...]
    high[own, :] = own_high[...]
    total[own, :] = own_sum[...]
    near_fetch.wait()
    far_fetch.wait()
    prefix_part(plan_ref, length_ref, near_cache, far_cache, heads_ref, acc, high, total)
    write_parts(sent_ref, acc, high, total)


def combine_kernel(parts_ref, out_ref):
    sources, heads_kv, rows, _ = parts_ref.shape
    for group in range(heads_kv):
        pieces = []
        for source in range(0, sources, 2):
            stat = jnp.concatenate(
                [parts_ref[source + i, group, :, WIDTH:].astype(jnp.float32) for i in range(2)],
                axis=0,
            )
            pieces.append([stat[:, place * GROUP : (place + 1) * GROUP] for place in range(5)])
        best = pieces[0][0]
        for coarse, *_ in pieces[1:]:
            best = jnp.maximum(best, coarse)
        best = jnp.maximum(best[:rows], best[rows:])
        best = jnp.concatenate([best, best], axis=0)
        shares = [
            jnp.exp(coarse - best + (middle + fine + last))
            for coarse, middle, fine, last, _ in pieces
        ]
        denom = shares[0]
        for share in shares[1:]:
            denom = denom + share
        denom = denom[:rows] + denom[rows:]
        denom = jnp.concatenate([denom, denom], axis=0) * SPREAD
        factors = [
            share * jnp.exp2(power) / denom for share, (*_, power) in zip(shares, pieces)
        ]
        for head in range(GROUP):
            columns = slice(head * HEAD_SIZE, (head + 1) * HEAD_SIZE)
            result = 0.0
            for pair, factor in enumerate(factors):
                coded = jnp.concatenate(
                    [
                        parts_ref[2 * pair + i, group, :, columns].astype(jnp.float32)
                        for i in range(2)
                    ],
                    axis=0,
                )
                result = result + factor[:, head : head + 1] * jnp.log(coded)
            start = group * WIDTH + head * HEAD_SIZE
            out_ref[:, start : start + HEAD_SIZE] = (result[:rows] + result[rows:]).astype(
                jnp.bfloat16
            )


def shards(
    queries, paths, node_owner, node_len, suf_len, prefix_kv, suffix_key_value, fresh_key_value
):
    x, z, core, kv = [lax.axis_index(name) for name in AXES]
    xs, zs, cores, kvs = [lax.axis_size(name) for name in AXES]
    rows_each = queries.shape[0]
    request_count = paths.shape[0]
    requests = zs * request_count
    smem = pl.BlockSpec(memory_space=pltpu.SMEM)
    vmem = pl.BlockSpec(memory_space=pltpu.VMEM)
    anywhere = pl.BlockSpec(memory_space=pl.ANY)

    def exchange(slabs):
        return lax.all_to_all(slabs, ("z", "kv"), split_axis=0, concat_axis=0, tiled=True)

    with jax.named_scope("send_queries"):
        outgoing = pl.pallas_call(
            pack_kernel,
            out_shape=jax.ShapeDtypeStruct((zs * kvs, rows_each, PAD_WIDTH), jnp.bfloat16),
            in_specs=[smem] * 3 + [vmem],
            out_specs=vmem,
            name="pack_queries",
        )(kv[None], paths.T, node_owner, queries)
        outgoing, own_cache = lax.optimization_barrier((outgoing, prefix_kv))
    with jax.named_scope("send_prefix"):
        ring = [own_cache]
        for step in SWAPS[1:]:
            ring.append(lax.ppermute(own_cache, "x", [(i, i ^ step) for i in range(xs)]))
        near = jnp.concatenate(ring, axis=0)
        far = lax.ppermute(near, "core", [(0, 1), (1, 0)])
    with jax.named_scope("send_queries"):
        received = exchange(outgoing)
        received = received.reshape(requests, PAD_WIDTH)
    with jax.named_scope("attend"):
        node_ids = lax.iota(jnp.int32, node_len.shape[0])
        chip = x ^ jnp.array(SWAPS, jnp.int32)
        held = jnp.concatenate([(chip * zs + z) * cores + lane for lane in (core, cores - 1 - core)])
        lengths = jnp.sum(jnp.where(held[:, None] == node_ids, node_len, 0), axis=-1)
        length = suffix_key_value.shape[2]
        valid = (lax.iota(jnp.int32, length)[None, :] < suf_len[:, None]).astype(jnp.int32)
        all_rows = ((requests + 1) * GROUP, HEAD_SIZE)
        own_rows = (request_count * GROUP, HEAD_SIZE)
        own = lax.dynamic_slice_in_dim(received, z * request_count, request_count, 0)
        own_part = jax.ShapeDtypeStruct(own_rows, jnp.float32)
        plan, heads = pl.pallas_call(
            plan_kernel,
            out_shape=(
                jax.ShapeDtypeStruct((xs * cores, LANES), jnp.int32),
                jax.ShapeDtypeStruct(all_rows, jnp.float32),
            ),
            in_specs=[smem, vmem],
            out_specs=[vmem] * 2,
            cost_estimate=pl.CostEstimate(
                flops=1 << 34, bytes_accessed=1 << 22, transcendentals=0
            ),
            compiler_params=pltpu.CompilerParams(vmem_limit_bytes=32 * 1024 * 1024),
            name="plan_requests",
        )(held, received)
        plan, own = lax.optimization_barrier((plan, own))
        own_parts = pl.pallas_call(
            local_kernel,
            out_shape=(own_part, own_part, own_part),
            in_specs=[vmem] * 4,
            out_specs=[vmem] * 3,
            scratch_shapes=[pltpu.VMEM(own_rows, jnp.float32)],
            compiler_params=pltpu.CompilerParams(vmem_limit_bytes=32 * 1024 * 1024),
            name="local_attention",
        )(
            own, fresh_key_value.transpose(1, 0, 2), valid.reshape(-1, 8 * length),
            suffix_key_value,
        )
        sent = pl.pallas_call(
            prefix_kernel,
            out_shape=jax.ShapeDtypeStruct((requests, PAD_WIDTH), jnp.bfloat16),
            in_specs=[smem] * 3 + [vmem] * 4 + [anywhere] * 2,
            out_specs=vmem,
            scratch_shapes=[pltpu.VMEM(all_rows, jnp.float32)] * 3
            + [pltpu.VMEM(near.shape, jnp.bfloat16)] * 2
            + [pltpu.SemaphoreType.DMA] * 2,
            compiler_params=pltpu.CompilerParams(vmem_limit_bytes=40 * 1024 * 1024),
            name="prefix_attention",
        )(plan, lengths, z[None], heads, *own_parts, near, far)
    with jax.named_scope("send_parts"):
        parts = exchange(sent.reshape(zs * kvs, rows_each, PAD_WIDTH))
        parts = parts.reshape(zs, kvs, rows_each, PAD_WIDTH)
    with jax.named_scope("combine"):
        return pl.pallas_call(
            combine_kernel,
            out_shape=jax.ShapeDtypeStruct((rows_each, kvs * WIDTH), jnp.bfloat16),
            compiler_params=pltpu.CompilerParams(vmem_limit_bytes=32 * 1024 * 1024),
            name="combine",
        )(parts)


def solution(mesh):
    owners, kvs = mesh.devices.shape
    split = Mesh(mesh.devices.reshape(4, 8, 2, kvs), AXES)
    return jax.shard_map(
        shards,
        mesh=split,
        in_specs=(
            P(AXES, None),
            P(OWNER, None),
            P(),
            P(),
            P(OWNER),
            P(OWNER, None, None, "kv"),
            P(OWNER, None, None, "kv"),
            P(OWNER, None, "kv"),
        ),
        out_specs=P(AXES, None),
        check_vma=False,
    )
```
